32 devices in a mesh: ctx: 32 (over z, y, x, core), head: 1.
Axes of the slice: x: 2, y: 2, z: 4, core: 2. Of those that a mesh axis runs over, the one named last changes fastest.
Arguments:
- query_rows: bfloat16 [8192, 1024], P('ctx', 'head'), may hold values from -6 to 6
- key_rows: bfloat16 [8192, 1024], P('ctx', 'head')
- value_rows: bfloat16 [8192, 1024], P('ctx', 'head'), may hold values from -6 to 6
- beta: float32 [8192, 8], P('ctx', 'head'), may hold values from 0 to 2
- norm_gain: float32 [128], replicated, may hold values from 0.1 to 1.9
- out_cotangent: bfloat16 [8192, 4096], P('ctx', 'head'), may hold values from -0.125 to 0.125
Outputs:
- attended: bfloat16 [8192, 1024], P('ctx', 'head')
- weight_grad: float32 [4096, 1024], P('ctx', 'head')
The draws below stay inside these ranges and needn't reach their ends.
All inputs are finite; a program needn't handle non-finite values.
Results may differ from the reference program's by a relative error of at most 0.0029.
Values may be sent and summed in bfloat16 or wider, within the bound.
A program may use at most 128 MiB of HBM per device.

```python
import math
import jax
import jax.numpy as jnp
from jax import lax

D = 4096
FEATURE_WIDTHS = 128
GROUP = 64
TOK_DEV = 256
ATTENTION_UNITS = 8
STEP_TOTAL = 8192


def draw_key_rows(key, part):
    streams = jax.random.split(jax.random.fold_in(key, 11), 3)
    result = jax.random.normal(streams[2], (STEP_TOTAL, ATTENTION_UNITS * FEATURE_WIDTHS))
    return result.astype(jnp.float32).astype(jnp.bfloat16)


def draw_beta(key, part):
    parallel_series = jax.random.split(key, 6)
    blocks = STEP_TOTAL // TOK_DEV
    order = jax.random.permutation(parallel_series[0], ATTENTION_UNITS)
    slow_count = ATTENTION_UNITS // 2
    slow = (order < slow_count).astype(jnp.float32)
    factor = jnp.exp(jax.random.uniform(parallel_series[1], (blocks, ATTENTION_UNITS), minval=math.log(0.5), maxval=math.log(2.0)))
    factor_rows = jnp.repeat(factor, TOK_DEV, axis=0)
    rough = jax.random.uniform(parallel_series[2], (STEP_TOTAL, ATTENTION_UNITS), minval=0.5, maxval=1.5)
    small = FEATURE_WIDTHS / STEP_TOTAL * factor_rows * rough
    slow_beta = 2.0 - small
    fast_beta = jax.random.uniform(parallel_series[3], (STEP_TOTAL, ATTENTION_UNITS), minval=0.3, maxval=1.7)
    mixture_beta_level = slow[None, :] * slow_beta + (1.0 - slow[None, :]) * fast_beta
    beginning_indices = jax.random.randint(parallel_series[4], (3,), 0, STEP_TOTAL - FEATURE_WIDTHS // 4)
    element_place = jnp.arange(STEP_TOTAL)[:, None]
    element_spike = jnp.any((element_place >= beginning_indices[None, :]) & (element_place < beginning_indices[None, :] + FEATURE_WIDTHS // 4), axis=1)
    spike_beta_level = jax.random.uniform(parallel_series[5], (STEP_TOTAL, ATTENTION_UNITS), minval=0.6, maxval=1.4)
    return jnp.where(element_spike[:, None], spike_beta_level, mixture_beta_level).astype(jnp.float32)


def strengthened(array, key, source, target, blocks, factor):
    def block_of(dim):
        return (jnp.arange(array.shape[dim]) // (array.shape[dim] // blocks)).reshape((-1,) + (1,) * (array.ndim - 1 - dim))

    first = jax.random.permutation(key, blocks)[block_of(target)]
    far = (block_of(target) + blocks // 2) % blocks
    return jnp.where((block_of(source) == first) | (block_of(source) == far), factor * array, array)


def block_scale(stream_key, extent, cuts, low, high):
    def one(dim, parts):
        steps = jax.random.uniform(jax.random.fold_in(jax.random.fold_in(stream_key, 6), dim), (parts,), jnp.float32, low / len(cuts), high / len(cuts))
        return jnp.repeat(jnp.exp(steps), extent[dim] // parts).reshape((-1,) + (1,) * (len(extent) - dim - 1))

    gain = one(*cuts[0])
    for cut in cuts[1:]:
        gain = gain * one(*cut)
    return gain


def gaussian(own_key, dims, deviation, limit, cuts=(), held_as=jnp.bfloat16):
    values = jax.random.normal(own_key, dims, jnp.float32) * deviation
    if len(cuts) > 0:
        values = block_scale(own_key, dims, cuts, -0.22, 0.18) * values
    return jnp.clip(values, min=-limit, max=limit).astype(held_as)


def bell_draw_with(rng, dims, deviation, most, shards, heavy, kind=jnp.bfloat16):
    values = deviation * jax.random.normal(rng, dims, jnp.float32)
    if shards:
        values = values * block_scale(rng, dims, shards, -0.22, 0.18)
    return jnp.clip(strengthened(values, jax.random.fold_in(rng, 3), *heavy), -most, most).astype(kind)


def setup_inputs(seed: int = 0) -> dict:
    arg_keys = jax.random.split(jax.random.key(seed), 7)
    query_rows = gaussian(arg_keys[0], (STEP_TOTAL, ATTENTION_UNITS * FEATURE_WIDTHS), 1.0, 6.0, ((0, 32),))
    key_rows = draw_key_rows(jax.random.fold_in(arg_keys[6], 71), 0)
    value_rows = gaussian(arg_keys[2], (STEP_TOTAL, ATTENTION_UNITS * FEATURE_WIDTHS), 1.0, 6.0, ((0, 32),))
    beta = draw_beta(jax.random.fold_in(arg_keys[6], 71), 0)
    norm_gain = jnp.clip(1.0 + 0.18 * jax.random.normal(arg_keys[4], (FEATURE_WIDTHS,), jnp.float32), 0.1, 1.9)
    out_cotangent = bell_draw_with(arg_keys[5], (STEP_TOTAL, D), (STEP_TOTAL ** -0.5), 0.125, ((0, 32),), (0, 1, 32, 2.75))
    return {"query_rows": query_rows, "key_rows": key_rows, "value_rows": value_rows, "beta": beta, "norm_gain": norm_gain, "out_cotangent": out_cotangent}


epsilon = 1e-06
highest = lax.Precision.HIGHEST

def matmul(pattern, former, latter):
    return jnp.einsum(pattern, former, latter, precision=highest, preferred_element_type=jnp.float32)

def unit_lower_inverse(strict_lower):
    negated = -strict_lower
    inverse = jnp.eye(GROUP, dtype=jnp.float32) + negated
    power = negated
    doubling = 2
    while doubling < GROUP:
        power = matmul('...ij,...jk->...ik', power, power)
        inverse = matmul('...ij,...jk->...ik', inverse, jnp.eye(GROUP, dtype=jnp.float32) + power)
        doubling = doubling * 2
    return inverse

def reference(query_rows, key_rows, value_rows, beta, norm_gain, out_cotangent):
    tok_total = query_rows.shape[0]
    heads = beta.shape[1]
    groups = tok_total // GROUP
    lower_mask = jnp.tril(jnp.ones((GROUP, GROUP), jnp.float32), -1)
    causal_mask = jnp.tril(jnp.ones((GROUP, GROUP), jnp.float32))

    def heads_view(block):
        return block.astype(jnp.float32).reshape(GROUP, heads, FEATURE_WIDTHS).transpose(1, 0, 2)

    def advance(state, pieces):
        query_block, key_block, value_block, beta_block = pieces
        query_f = heads_view(query_block)
        key_raw = heads_view(key_block)
        key_unit = key_raw * lax.rsqrt(lax.optimization_barrier(jnp.sum(key_raw * key_raw, axis=-1, keepdims=True)) + epsilon)
        value_f = heads_view(value_block)
        strength = beta_block.T[:, :, None]
        inverse = unit_lower_inverse(lower_mask * (strength * matmul('hid,hjd->hij', key_unit, key_unit)))
        stacked = jnp.concatenate([strength * key_unit, strength * value_f], axis=-1)
        solved = matmul('hij,hjd->hid', inverse, stacked)
        corrected = solved[..., FEATURE_WIDTHS:] - matmul('hcd,hde->hce', solved[..., :FEATURE_WIDTHS], state)
        scores = causal_mask * matmul('hid,hjd->hij', query_f, key_unit)
        mixed = matmul('hcd,hde->hce', query_f, state) + matmul('hij,hje->hie', scores, corrected)
        new_state = state + matmul('hcd,hce->hde', key_unit, corrected)
        mean_square = lax.optimization_barrier(jnp.mean(mixed * mixed, axis=-1, keepdims=True))
        normed = mixed * lax.rsqrt(mean_square + epsilon) * norm_gain
        return (new_state, normed.astype(jnp.bfloat16).transpose(1, 0, 2).reshape(GROUP, heads * FEATURE_WIDTHS))
    start = jnp.zeros((heads, FEATURE_WIDTHS, FEATURE_WIDTHS), jnp.float32)
    pieces = (query_rows.reshape(groups, GROUP, heads * FEATURE_WIDTHS), key_rows.reshape(groups, GROUP, heads * FEATURE_WIDTHS), value_rows.reshape(groups, GROUP, heads * FEATURE_WIDTHS), beta.reshape(groups, GROUP, heads))
    final_state, outputs = lax.scan(advance, start, pieces)
    attended = outputs.reshape(tok_total, heads * FEATURE_WIDTHS)
    weight_grad = jnp.dot(out_cotangent.T, attended, preferred_element_type=jnp.float32)
    return (attended, weight_grad)
```

```python
import functools

import jax
import jax.numpy as jnp
from jax import lax
from jax.experimental import pallas as pl
from jax.experimental.pallas import tpu as pltpu
from jax.sharding import PartitionSpec as P

EPS = 1e-06
CORES = 2
F32 = jnp.float32
BF16 = jnp.bfloat16


def dot(a, b):
    return lax.dot_general(a, b, (((1,), (0,)), ((), ())), preferred_element_type=F32)


def dot_nt(a, b):
    return lax.dot_general(a, b, (((1,), (1,)), ((), ())), preferred_element_type=F32)


def dot_tn(a, b):
    return lax.dot_general(a, b, (((0,), (0,)), ((), ())), preferred_element_type=F32)


def halves(x):
    hi = x.astype(BF16)
    return hi, (x - hi.astype(F32)).astype(BF16)


def mm_packed(a, b):
    n = b.shape[1]
    ah, al = halves(a)
    bh, bl = halves(b)
    left = jnp.concatenate([ah, al], axis=1)
    right = jnp.concatenate(
        [jnp.concatenate([bh, bl], axis=1), jnp.concatenate([bh, jnp.zeros_like(bl)], axis=1)],
        axis=0,
    )
    both = dot(left, right)
    return both[:, :n] + both[:, n:]


def mm3(a, b):
    ah, al = halves(a)
    bh, bl = halves(b)
    return dot(ah, bh) + (dot(ah, bl) + dot(al, bh))


def mm_tall(a, b):
    ah, al = halves(a)
    bh, bl = halves(b)
    left = jnp.concatenate([ah, al], axis=1)
    return dot(left, jnp.concatenate([bh, bh], axis=0)) + dot(ah, bl)


def chunk_inverse(lower, tok, block):
    row = lax.broadcasted_iota(jnp.int32, (block, block), 0)
    col = lax.broadcasted_iota(jnp.int32, (block, block), 1)
    apart = row ^ col
    eye = (row == col).astype(F32)
    diag = []
    for b in range(tok // block):
        part = lower[b * block : (b + 1) * block, b * block : (b + 1) * block]
        inv = eye - jnp.where(apart < 2, part, 0.0)
        diag.append((part, inv))
    size = 2
    while size < block:
        pick = (apart >= size) & (apart < 2 * size)
        diag = [
            (part, inv - mm_packed(mm_packed(inv, jnp.where(pick, part, 0.0)), inv))
            for part, inv in diag
        ]
        size *= 2
    return [inv for _, inv in diag]


def local_head(qb, kb, vb, strength, tok, width):
    block = min(tok, width)
    row = lax.broadcasted_iota(jnp.int32, (tok, tok), 0)
    col = lax.broadcasted_iota(jnp.int32, (tok, tok), 1)
    gram = dot_nt(kb, kb)
    onto = jnp.where(row == col, gram, 0.0)
    r_col = lax.rsqrt(jnp.sum(onto, axis=1, keepdims=True) + EPS)
    r_row = lax.rsqrt(jnp.sum(onto, axis=0, keepdims=True) + EPS)
    lower = jnp.where(row > col, gram * (strength * r_col) * r_row, 0.0)
    invs = chunk_inverse(lower, tok, block)
    kf = kb.astype(F32)
    rhs = jnp.concatenate([kf * (strength * r_col), vb.astype(F32) * strength], axis=1)
    solved = []
    for b in range(tok // block):
        want = rhs[b * block : (b + 1) * block]
        if b > 0:
            want = want - mm3(
                lower[b * block : (b + 1) * block, : b * block], jnp.concatenate(solved, axis=0)
            )
        solved.append(mm_tall(invs[b], want))
    y = jnp.concatenate(solved, axis=0)
    yh, yl = halves(y * r_col)
    kty = dot_tn(kb, yh) + dot_tn(kb, yl)
    frow = lax.broadcasted_iota(jnp.int32, (width, 2 * width), 0)
    fcol = lax.broadcasted_iota(jnp.int32, (width, 2 * width), 1)
    tw = jnp.where(fcol < width, (frow == fcol).astype(F32) - kty, kty)
    scores = jnp.where(row >= col, dot_nt(qb, kb) * r_row, 0.0)
    sy = mm3(scores, y)
    cb = jnp.concatenate([qb.astype(F32) - sy[:, :width], sy[:, width:]], axis=1)
    return tw, cb


def kernel(
    dims,
    q_ref,
    k_ref,
    v_ref,
    beta_ref,
    gain_ref,
    cot_ref,
    att_ref,
    wg_ref,
    cotr,
    cott,
    tw,
    twr,
    cb,
    pre,
    sz,
    snext,
    st_send,
    st,
    attg,
    rs_s,
    rs_r,
    own,
    cot_own_sem,
    cota_s,
    cota_r,
    cotb_s,
    cotb_r,
    tw_s,
    tw_r,
    sz_s,
    sz_r,
    st_s,
    st_r,
    att_s,
    att_r,
    rs_ss,
    rs_rs,
):
    total, planes, group, chips, heads, tok, width, rows, steps = dims
    me = lax.axis_index("ctx")
    z = me // group
    j = me % group
    m = j // CORES
    c = j % CORES
    sib = 1 - c
    cw = CORES * rows
    half = heads * width // CORES
    uw = half // steps

    def remote(src, dst, ssem, rsem, target):
        return pltpu.make_async_remote_copy(
            src_ref=src,
            dst_ref=dst,
            send_sem=ssem,
            recv_sem=rsem,
            device_id={"ctx": target},
            device_id_type=pl.DeviceIdType.MESH,
        )

    barrier = pltpu.get_barrier_semaphore()
    peers = [z * group + (j + k) % group for k in range(1, group)]
    for kz in range(1, planes):
        zz = (z + kz) % planes
        peers += [zz * group + m * CORES + c, zz * group + m * CORES + sib]
    for peer in peers:
        pl.semaphore_signal(
            barrier, inc=1, device_id={"ctx": peer}, device_id_type=pl.DeviceIdType.MESH
        )
    pl.semaphore_wait(barrier, len(peers))

    def cot_cols(zz, mm):
        return cot_ref.at[:, pl.ds(pl.multiple_of((zz * group + mm * CORES) * rows, cw), cw)]

    def cot_a(k, zz):
        mm = (m + k) % chips
        return remote(
            cot_cols(zz, mm),
            cotr.at[j, zz],
            cota_s.at[k, zz],
            cota_r.at[k, zz],
            z * group + mm * CORES + c,
        )

    def cot_mine(zz):
        return pltpu.make_async_copy(cot_cols(zz, m), cotr.at[j, zz], cot_own_sem.at[zz])

    def cot_b(k, zz):
        source = ((m + chips - k) % chips) * CORES + c
        return remote(
            cotr.at[source, zz],
            cotr.at[source, zz],
            cotb_s.at[k, zz],
            cotb_r.at[k, zz],
            z * group + m * CORES + sib,
        )

    for zz in range(planes):
        cot_mine(zz).start()
    for k in range(1, chips):
        for zz in range(planes):
            cot_a(k, zz).start()

    def tw_copy(h, slot):
        return remote(tw.at[h], twr.at[slot], tw_s.at[h], tw_r.at[slot], z * group + h)

    lanes = lax.broadcasted_iota(jnp.int32, (tok, heads), 1)
    batch = 4 if heads % 4 == 0 else 1

    def some_heads(step, _):
        for b in range(batch):
            h = step * batch + b
            cols = pl.ds(pl.multiple_of(h * width, width), width)
            strength = jnp.sum(
                jnp.where(lanes == h, beta_ref[...], 0.0), axis=1, keepdims=True
            )
            got_tw, got_cb = local_head(
                q_ref[:, cols], k_ref[:, cols], v_ref[:, cols], strength, tok, width
            )
            tw[h] = got_tw
            cb[h] = got_cb
        for b in range(batch):
            h = step * batch + b

            @pl.when(h != j)
            def _():
                tw_copy(h, j).start()

        return 0

    lax.fori_loop(0, heads // batch, some_heads, 0)
    twr[j] = tw[j]

    for zz in range(planes):
        cot_mine(zz).wait()
        cot_b(0, zz).start()
    for k in range(1, group):
        tw_copy((j + k) % group, (j + k) % group).wait_recv()

    frow = lax.broadcasted_iota(jnp.int32, (width, 2 * width), 0)
    fcol = lax.broadcasted_iota(jnp.int32, (width, 2 * width), 1)
    pre[0] = (frow == fcol).astype(F32)

    def compose(i, _):
        pair = twr[i]
        pre[i + 1] = mm_tall(pair[:, :width], pre[i]) + jnp.where(fcol < width, 0.0, pair)
        return 0

    lax.fori_loop(0, group, compose, 0)

    def sz_copy(target):
        return remote(snext, sz, sz_s, sz_r, target)

    @pl.when(z == 0)
    def _():
        sz[...] = jnp.zeros_like(sz)

    @pl.when(z > 0)
    def _():
        sz_copy(me).wait_recv()

    state = sz[...]

    @pl.when(z < planes - 1)
    def _():
        pair = pre[group]
        snext[...] = mm_packed(pair[:, :width], state) + pair[:, width:]
        sz_copy(me + group).start()

    def st_copy(i, slot):
        return remote(st_send.at[i], st.at[slot], st_s.at[i], st_r.at[slot], z * group + i)

    for k in range(group):
        i = (j + k) % group
        pair = pre[i]
        st_send[i] = mm_packed(pair[:, :width], state) + pair[:, width:]
        if k > 0:
            st_copy(i, j).start()
    st[j] = st_send[j]

    for k in range(1, chips):
        for zz in range(planes):
            cot_a(k, zz).wait_recv()
            cot_b(k, zz).start()
    for k in range(chips):
        source = ((m + chips - k) % chips) * CORES + c
        at = pl.ds(pl.multiple_of(source * tok, tok), tok)
        for zz in range(planes):
            cott[zz, :, at] = cotr[source, zz].T

    gain = gain_ref[...]

    def att_copy(u, i, ci, slot, sem_s, sem_r):
        return remote(
            att_ref.at[:, pl.ds(pl.multiple_of(ci * half + u * uw, uw), uw)],
            attg.at[u, pl.ds(pl.multiple_of(slot * tok, tok), tok), :],
            att_s.at[u, sem_s],
            att_r.at[u, sem_r],
            z * group + i,
        )

    per = uw // width
    for u in range(steps):
        for ci in range(CORES):
            for e in range(per):
                h = ci * (heads // CORES) + u * per + e

                @pl.when(j != h)
                def _():
                    st_copy(j, h).wait_recv()

                pair = cb[h]
                mixed = pair[:, width:] + mm_packed(pair[:, :width], st[h])
                square = jnp.mean(mixed * mixed, axis=1, keepdims=True)
                att_ref[:, h * width : (h + 1) * width] = (
                    mixed * lax.rsqrt(square + EPS) * gain
                ).astype(BF16)
        for k in range(1, group):
            i = (j + k) % group
            att_copy(u, i, i % CORES, j, i, j).start()
        attg[u, pl.ds(pl.multiple_of(j * tok, tok), tok), :] = att_ref[
            :, pl.ds(pl.multiple_of(c * half + u * uw, uw), uw)
        ]

    for k in range(chips):
        source = ((m + chips - k) % chips) * CORES + sib
        at = pl.ds(pl.multiple_of(source * tok, tok), tok)
        for zz in range(planes):
            remote(
                cotr.at[source, zz],
                cotr.at[source, zz],
                cotb_s.at[k, zz],
                cotb_r.at[k, zz],
                me,
            ).wait_recv()
            cott[zz, :, at] = cotr[source, zz].T

    def rs_copy(u, zz, cc, zs, cs):
        return remote(
            rs_s.at[u, zz, pl.ds(pl.multiple_of(cc * rows, rows), rows), :],
            rs_r.at[u, zs, cs],
            rs_ss.at[u, zz, cc],
            rs_rs.at[u, zs, cs],
            zz * group + m * CORES + cc,
        )

    for u in range(steps):
        for k in range(1, group):
            i = (j + k) % group
            att_copy(u, i, c, i, i, i).wait_recv()
        for kz in list(range(1, planes)) + [0]:
            zz = (z + kz) % planes
            part = dot(cott[zz], attg[u])
            rs_s[u, zz] = part.astype(BF16)
            if kz == 0:
                own[u] = part
                rs_copy(u, zz, sib, z, c).start()
            else:
                rs_copy(u, zz, c, z, c).start()
                rs_copy(u, zz, sib, z, c).start()

    for u in range(steps):
        acc = own[u, pl.ds(pl.multiple_of(c * rows, rows), rows), :]
        for kz in range(1, planes):
            zz = (z + kz) % planes
            rs_copy(u, z, c, zz, c).wait_recv()
            acc = acc + rs_r[u, zz, c].astype(F32)
        wg_ref[:, pl.ds(pl.multiple_of(c * half + u * uw, uw), uw)] = acc
        acc = jnp.zeros((rows, uw), F32)
        for kz in range(planes):
            zz = (z + kz) % planes
            rs_copy(u, z, c, zz, sib).wait_recv()
            acc = acc + rs_r[u, zz, sib].astype(F32)
        wg_ref[:, pl.ds(pl.multiple_of(sib * half + u * uw, uw), uw)] = acc

    for zz in range(planes):
        for k in range(1, chips):
            cot_a(k, zz).wait_send()
        for k in range(chips):
            cot_b(k, zz).wait_send()
    for k in range(1, group):
        i = (j + k) % group
        tw_copy(i, j).wait_send()
        st_copy(i, j).wait_send()
        for u in range(steps):
            att_copy(u, i, i % CORES, j, i, j).wait_send()

    @pl.when(z < planes - 1)
    def _():
        sz_copy(me + group).wait_send()

    for u in range(steps):
        for kz in range(planes):
            zz = (z + kz) % planes
            if kz > 0:
                rs_copy(u, zz, c, z, c).wait_send()
            rs_copy(u, zz, sib, z, c).wait_send()


def on_device(total, joined, query_rows, key_rows, value_rows, beta, norm_gain, out_cotangent):
    tok = query_rows.shape[0]
    heads = beta.shape[1]
    width = query_rows.shape[1] // heads
    if joined > 1:
        out_cotangent = lax.all_gather(out_cotangent, "head", axis=1, tiled=True)
    model = out_cotangent.shape[1]
    rows = model // total
    group = heads
    planes = total // group
    chips = group // CORES
    steps = 2
    half = heads * width // CORES
    uw = half // steps
    dims = (total, planes, group, chips, heads, tok, width, rows, steps)
    vmem = pl.BlockSpec(memory_space=pltpu.VMEM)
    dma = pltpu.SemaphoreType.DMA
    return pl.pallas_call(
        functools.partial(kernel, dims),
        out_shape=(
            jax.ShapeDtypeStruct((tok, heads * width), BF16),
            jax.ShapeDtypeStruct((rows, heads * width), F32),
        ),
        in_specs=[vmem] * 5 + [pl.BlockSpec(memory_space=pl.ANY)],
        out_specs=(vmem, vmem),
        scratch_shapes=[
            pltpu.VMEM((group, planes, tok, CORES * rows), BF16),
            pltpu.VMEM((planes, CORES * rows, group * tok), BF16),
            pltpu.VMEM((heads, width, 2 * width), F32),
            pltpu.VMEM((group, width, 2 * width), F32),
            pltpu.VMEM((heads, tok, 2 * width), F32),
            pltpu.VMEM((group + 1, width, 2 * width), F32),
            pltpu.VMEM((width, width), F32),
            pltpu.VMEM((width, width), F32),
            pltpu.VMEM((group, width, width), F32),
            pltpu.VMEM((heads, width, width), F32),
            pltpu.VMEM((steps, group * tok, uw), BF16),
            pltpu.VMEM((steps, planes, CORES * rows, uw), BF16),
            pltpu.VMEM((steps, planes, CORES, rows, uw), BF16),
            pltpu.VMEM((steps, CORES * rows, uw), F32),
            dma((planes,)),
            dma((chips, planes)),
            dma((chips, planes)),
            dma((chips, planes)),
            dma((chips, planes)),
            dma((heads,)),
            dma((heads,)),
            dma,
            dma,
            dma((group,)),
            dma((heads,)),
            dma((steps, group)),
            dma((steps, group)),
            dma((steps, planes, CORES)),
            dma((steps, planes, CORES)),
        ],
        compiler_params=pltpu.CompilerParams(
            collective_id=0, has_side_effects=True, vmem_limit_bytes=56 * 1024 * 1024
        ),
    )(query_rows, key_rows, value_rows, beta, norm_gain.reshape(1, -1), out_cotangent)


def solution(mesh):
    spec = P("ctx", "head")
    return jax.shard_map(
        functools.partial(on_device, mesh.shape["ctx"], mesh.shape["head"]),
        mesh=mesh,
        in_specs=(spec, spec, spec, spec, P(), spec),
        out_specs=(spec, spec),
        check_vma=False,
    )
```

```python
import functools

import jax
import jax.numpy as jnp
from jax import lax
from jax.experimental import pallas as pl
from jax.experimental.pallas import tpu as pltpu
from jax.sharding import PartitionSpec as P

EPS = 1e-06
CORES = 2
F32 = jnp.float32
BF16 = jnp.bfloat16


def dot(a, b):
    return lax.dot_general(a, b, (((1,), (0,)), ((), ())), preferred_element_type=F32)


def dot_nt(a, b):
    return lax.dot_general(a, b, (((1,), (1,)), ((), ())), preferred_element_type=F32)


def dot_tn(a, b):
    return lax.dot_general(a, b, (((0,), (0,)), ((), ())), preferred_element_type=F32)


def halves(x):
    hi = x.astype(BF16)
    return hi, (x - hi.astype(F32)).astype(BF16)


def mm_packed(a, b):
    n = b.shape[1]
    ah, al = halves(a)
    bh, bl = halves(b)
    left = jnp.concatenate([ah, al], axis=1)
    right = jnp.concatenate(
        [jnp.concatenate([bh, bl], axis=1), jnp.concatenate([bh, jnp.zeros_like(bl)], axis=1)],
        axis=0,
    )
    both = dot(left, right)
    return both[:, :n] + both[:, n:]


def mm3(a, b):
    ah, al = halves(a)
    bh, bl = halves(b)
    return dot(ah, bh) + (dot(ah, bl) + dot(al, bh))


def mm_tall(a, b):
    ah, al = halves(a)
    bh, bl = halves(b)
    left = jnp.concatenate([ah, al], axis=1)
    return dot(left, jnp.concatenate([bh, bh], axis=0)) + dot(ah, bl)


def chunk_inverse(lower, tok, block):
    row = lax.broadcasted_iota(jnp.int32, (block, block), 0)
    col = lax.broadcasted_iota(jnp.int32, (block, block), 1)
    apart = row ^ col
    eye = (row == col).astype(F32)
    diag = []
    for b in range(tok // block):
        part = lower[b * block : (b + 1) * block, b * block : (b + 1) * block]
        inv = eye - jnp.where(apart < 2, part, 0.0)
        diag.append((part, inv))
    size = 2
    while size < block:
        pick = (apart >= size) & (apart < 2 * size)
        diag = [
            (part, inv - mm_packed(mm_packed(inv, jnp.where(pick, part, 0.0)), inv))
            for part, inv in diag
        ]
        size *= 2
    return [inv for _, inv in diag]


def local_head(qb, kb, vb, strength, tok, width):
    block = min(tok, width)
    row = lax.broadcasted_iota(jnp.int32, (tok, tok), 0)
    col = lax.broadcasted_iota(jnp.int32, (tok, tok), 1)
    gram = dot_nt(kb, kb)
    onto = jnp.where(row == col, gram, 0.0)
    r_col = lax.rsqrt(jnp.sum(onto, axis=1, keepdims=True) + EPS)
    r_row = lax.rsqrt(jnp.sum(onto, axis=0, keepdims=True) + EPS)
    lower = jnp.where(row > col, gram * (strength * r_col) * r_row, 0.0)
    invs = chunk_inverse(lower, tok, block)
    kf = kb.astype(F32)
    rhs = jnp.concatenate([kf * (strength * r_col), vb.astype(F32) * strength], axis=1)
    solved = []
    for b in range(tok // block):
        want = rhs[b * block : (b + 1) * block]
        if b > 0:
            want = want - mm3(
                lower[b * block : (b + 1) * block, : b * block], jnp.concatenate(solved, axis=0)
            )
        solved.append(mm_tall(invs[b], want))
    y = jnp.concatenate(solved, axis=0)
    yh, yl = halves(y * r_col)
    kty = dot_tn(kb, yh) + dot_tn(kb, yl)
    frow = lax.broadcasted_iota(jnp.int32, (width, 2 * width), 0)
    fcol = lax.broadcasted_iota(jnp.int32, (width, 2 * width), 1)
    tw = jnp.where(fcol < width, (frow == fcol).astype(F32) - kty, kty)
    scores = jnp.where(row >= col, dot_nt(qb, kb) * r_row, 0.0)
    sy = mm3(scores, y)
    cb = jnp.concatenate([qb.astype(F32) - sy[:, :width], sy[:, width:]], axis=1)
    return tw, cb


def kernel(
    dims,
    q_ref,
    k_ref,
    v_ref,
    beta_ref,
    gain_ref,
    cot_ref,
    att_ref,
    wg_ref,
    cotr,
    att_t,
    tw,
    twr,
    cb,
    pre,
    tree,
    zp,
    sz,
    snext,
    scur,
    st_send,
    st,
    attg,
    rs_s,
    rs_r,
    own,
    cot_own_sem,
    cota_s,
    cota_r,
    cotb_s,
    cotb_r,
    tw_s,
    tw_r,
    zp_s,
    zp_r,
    sz_s,
    sz_r,
    st_s,
    st_r,
    att_s,
    att_r,
    rs_ss,
    rs_rs,
):
    total, planes, group, chips, heads, tok, width, rows, steps = dims
    me = lax.axis_index("ctx")
    z = me // group
    j = me % group
    m = j // CORES
    c = j % CORES
    sib = 1 - c
    cw = CORES * rows
    half = heads * width // CORES
    uw = half // steps

    def remote(src, dst, ssem, rsem, target):
        return pltpu.make_async_remote_copy(
            src_ref=src,
            dst_ref=dst,
            send_sem=ssem,
            recv_sem=rsem,
            device_id={"ctx": target},
            device_id_type=pl.DeviceIdType.MESH,
        )

    barrier = pltpu.get_barrier_semaphore()
    peers = [z * group + (j + k) % group for k in range(1, group)]
    for kz in range(1, planes):
        zz = (z + kz) % planes
        peers += [zz * group + m * CORES + c, zz * group + m * CORES + sib]
    for peer in peers:
        pl.semaphore_signal(
            barrier, inc=1, device_id={"ctx": peer}, device_id_type=pl.DeviceIdType.MESH
        )
    pl.semaphore_wait(barrier, len(peers))

    def cot_cols(zz, mm):
        return cot_ref.at[:, pl.ds(pl.multiple_of((zz * group + mm * CORES) * rows, cw), cw)]

    def came(source, zz):
        return cotr.at[zz, pl.ds(pl.multiple_of(source * tok, tok), tok), :]

    def cot_a(k, zz):
        mm = (m + k) % chips
        return remote(
            cot_cols(zz, mm),
            came(j, zz),
            cota_s.at[k, zz],
            cota_r.at[k, zz],
            z * group + mm * CORES + c,
        )

    def cot_mine(zz):
        return pltpu.make_async_copy(cot_cols(zz, m), came(j, zz), cot_own_sem.at[zz])

    def cot_b(k, zz):
        source = ((m + chips - k) % chips) * CORES + c
        return remote(
            came(source, zz),
            came(source, zz),
            cotb_s.at[k, zz],
            cotb_r.at[k, zz],
            z * group + m * CORES + sib,
        )

    for zz in range(planes):
        cot_mine(zz).start()
    for k in range(1, chips):
        for zz in range(planes):
            cot_a(k, zz).start()

    def tw_copy(h, slot):
        return remote(tw.at[h], twr.at[slot], tw_s.at[h], tw_r.at[slot], z * group + h)

    turn = lax.broadcasted_iota(jnp.int32, (tok, tok), 0) == lax.broadcasted_iota(
        jnp.int32, (tok, tok), 1
    )
    batch = 4 if heads % 4 == 0 else 1

    def some_heads(step, _):
        for b in range(batch):
            h = step * batch + b
            cols = pl.ds(pl.multiple_of(h * width, width), width)
            strength = jnp.sum(
                jnp.where(turn, beta_ref[pl.ds(h, 1), :], 0.0), axis=1, keepdims=True
            )
            got_tw, got_cb = local_head(
                q_ref[:, cols], k_ref[:, cols], v_ref[:, cols], strength, tok, width
            )
            tw[h] = got_tw
            cb[h] = got_cb
        for b in range(batch):
            h = step * batch + b

            @pl.when(h != j)
            def _():
                tw_copy(h, j).start()

        return 0

    lax.fori_loop(0, heads // batch, some_heads, 0)
    twr[j] = tw[j]

    for k in range(1, group):
        tw_copy((j + k) % group, (j + k) % group).wait_recv()

    frow = lax.broadcasted_iota(jnp.int32, (width, 2 * width), 0)
    fcol = lax.broadcasted_iota(jnp.int32, (width, 2 * width), 1)

    def compose(later, earlier):
        return mm_tall(later[:, :width], earlier) + jnp.where(fcol < width, 0.0, later)

    levels = [[twr.at[i] for i in range(group)]]
    used = 0
    while len(levels[-1]) > 1:
        below = levels[-1]
        above = [tree.at[used + i] for i in range(len(below) // 2)]
        for i, node in enumerate(above):
            node[...] = compose(below[2 * i + 1][...], below[2 * i][...])
        used += len(above)
        levels.append(above)
    top = tree.at[used - 1]

    def zp_copy(target):
        return remote(top, zp, zp_s, zp_r, target)

    def sz_copy(n, target):
        return remote(snext, sz, sz_s.at[n], sz_r, target)

    @pl.when((z % 2 == 0) & (z < planes - 1))
    def _():
        zp_copy(me + group).start()

    def odd_state():
        zp_copy(me).wait_recv()

        @pl.when(z == 1)
        def _():
            scur[...] = zp[:, width:]

        @pl.when(z > 1)
        def _():
            sz_copy(0, me).wait_recv()
            scur[...] = mm_packed(zp[:, :width], sz[...]) + zp[:, width:]

    @pl.when((z % 2 == 1) & (z < planes - 1))
    def _():
        odd_state()
        snext[...] = mm_packed(top[:, :width], scur[...]) + top[:, width:]
        sz_copy(0, me + group).start()

        @pl.when(z < planes - 2)
        def _():
            sz_copy(1, me + 2 * group).start()

    pre[0] = (frow == fcol).astype(F32)
    span = group // 2
    depth = len(levels) - 2
    while span >= 1:
        for i in range(0, group, 2 * span):
            node = levels[depth][i // span]
            if i == 0:
                pre[span] = node[...]
            else:
                pre[i + span] = compose(node[...], pre[i])
        span //= 2
        depth -= 1

    @pl.when((z % 2 == 1) & (z == planes - 1))
    def _():
        odd_state()

    @pl.when((z % 2 == 0) & (z > 0))
    def _():
        sz_copy(0, me).wait_recv()
        scur[...] = sz[...]

    @pl.when(z == 0)
    def _():
        scur[...] = jnp.zeros_like(scur)

    state = scur[...]

    def st_copy(i, slot):
        return remote(st_send.at[i], st.at[slot], st_s.at[i], st_r.at[slot], z * group + i)

    for k in range(1, group + 1):
        i = (j + k) % group
        pair = pre[i]
        st_send[i] = mm_packed(pair[:, :width], state) + pair[:, width:]
        if k < group:
            st_copy(i, j).start()
    st[j] = st_send[j]

    for k in range(chips):
        for zz in range(planes):
            if k == 0:
                cot_mine(zz).wait()
            else:
                cot_a(k, zz).wait_recv()
            cot_b(k, zz).start()

    gain = gain_ref[...]

    def att_copy(u, i, ci, slot, sem_s, sem_r):
        return remote(
            att_t.at[u, ci],
            attg.at[u, :, pl.ds(pl.multiple_of(slot * tok, tok), tok)],
            att_s.at[u, sem_s],
            att_r.at[u, sem_r],
            z * group + i,
        )

    per = uw // width
    for u in range(steps):
        for ci in range(CORES):
            for e in range(per):
                h = ci * (heads // CORES) + u * per + e

                @pl.when(j != h)
                def _():
                    st_copy(j, h).wait_recv()

                pair = cb[h]
                mixed = pair[:, width:] + mm_packed(pair[:, :width], st[h])
                square = jnp.mean(mixed * mixed, axis=1, keepdims=True)
                normed = mixed * lax.rsqrt(square + EPS) * gain
                att_ref[:, h * width : (h + 1) * width] = normed.astype(BF16)
                att_t[u, ci, e * width : (e + 1) * width, :] = normed.T.astype(BF16)
        for k in range(1, group):
            i = (j + k) % group
            att_copy(u, i, i % CORES, j, i, j).start()
        attg[u, :, pl.ds(pl.multiple_of(j * tok, tok), tok)] = att_t[u, c]

    for k in range(chips):
        source = ((m + chips - k) % chips) * CORES + sib
        for zz in range(planes):
            remote(
                came(source, zz),
                came(source, zz),
                cotb_s.at[k, zz],
                cotb_r.at[k, zz],
                me,
            ).wait_recv()

    def rs_copy(u, zz, cc, zs, cs):
        return remote(
            rs_s.at[u, zz, :, pl.ds(pl.multiple_of(cc * rows, rows), rows)],
            rs_r.at[u, zs, cs],
            rs_ss.at[u, zz, cc],
            rs_rs.at[u, zs, cs],
            zz * group + m * CORES + cc,
        )

    for u in range(steps):
        for k in range(1, group):
            i = (j + k) % group
            att_copy(u, i, c, i, i, i).wait_recv()
        for kz in list(range(1, planes)) + [0]:
            zz = (z + kz) % planes
            part = dot(attg[u], cotr[zz])
            rs_s[u, zz] = part.astype(BF16)
            if kz == 0:
                own[u] = part
                rs_copy(u, zz, sib, z, c).start()
            else:
                rs_copy(u, zz, c, z, c).start()
                rs_copy(u, zz, sib, z, c).start()

    for u in range(steps):
        acc = own[u, :, pl.ds(pl.multiple_of(c * rows, rows), rows)]
        for kz in range(1, planes):
            zz = (z + kz) % planes
            rs_copy(u, z, c, zz, c).wait_recv()
            acc = acc + rs_r[u, zz, c].astype(F32)
        wg_ref[:, pl.ds(pl.multiple_of(c * half + u * uw, uw), uw)] = acc.T
        acc = jnp.zeros((uw, rows), F32)
        for kz in range(planes):
            zz = (z + kz) % planes
            rs_copy(u, z, c, zz, sib).wait_recv()
            acc = acc + rs_r[u, zz, sib].astype(F32)
        wg_ref[:, pl.ds(pl.multiple_of(sib * half + u * uw, uw), uw)] = acc.T

    for zz in range(planes):
        for k in range(1, chips):
            cot_a(k, zz).wait_send()
        for k in range(chips):
            cot_b(k, zz).wait_send()
    for k in range(1, group):
        i = (j + k) % group
        tw_copy(i, j).wait_send()
        st_copy(i, j).wait_send()
        for u in range(steps):
            att_copy(u, i, i % CORES, j, i, j).wait_send()

    @pl.when((z % 2 == 0) & (z < planes - 1))
    def _():
        zp_copy(me + group).wait_send()

    @pl.when((z % 2 == 1) & (z < planes - 1))
    def _():
        sz_copy(0, me + group).wait_send()

        @pl.when(z < planes - 2)
        def _():
            sz_copy(1, me + 2 * group).wait_send()

    for u in range(steps):
        for kz in range(planes):
            zz = (z + kz) % planes
            if kz > 0:
                rs_copy(u, zz, c, z, c).wait_send()
            rs_copy(u, zz, sib, z, c).wait_send()


def hand_over(att_in, wg_in, att_out, wg_out):
    att_out[...] = att_in[...]
    wg_out[...] = wg_in[...]


def on_device(total, joined, query_rows, key_rows, value_rows, beta, norm_gain, out_cotangent):
    tok = query_rows.shape[0]
    heads = beta.shape[1]
    width = query_rows.shape[1] // heads
    if joined > 1:
        out_cotangent = lax.all_gather(out_cotangent, "head", axis=1, tiled=True)
    model = out_cotangent.shape[1]
    rows = model // total
    group = heads
    planes = total // group
    chips = group // CORES
    steps = 4
    half = heads * width // CORES
    uw = half // steps
    dims = (total, planes, group, chips, heads, tok, width, rows, steps)
    vmem = pl.BlockSpec(memory_space=pltpu.VMEM)
    dma = pltpu.SemaphoreType.DMA
    attended, weight_grad = pl.pallas_call(
        functools.partial(kernel, dims),
        out_shape=(
            jax.ShapeDtypeStruct((tok, heads * width), BF16),
            jax.ShapeDtypeStruct((rows, heads * width), F32),
        ),
        in_specs=[vmem] * 5 + [pl.BlockSpec(memory_space=pl.ANY)],
        out_specs=(vmem, vmem),
        scratch_shapes=[
            pltpu.VMEM((planes, group * tok, CORES * rows), BF16),
            pltpu.VMEM((steps, CORES, uw, tok), BF16),
            pltpu.VMEM((heads, width, 2 * width), F32),
            pltpu.VMEM((group, width, 2 * width), F32),
            pltpu.VMEM((heads, tok, 2 * width), F32),
            pltpu.VMEM((group, width, 2 * width), F32),
            pltpu.VMEM((group - 1, width, 2 * width), F32),
            pltpu.VMEM((width, 2 * width), F32),
            pltpu.VMEM((width, width), F32),
            pltpu.VMEM((width, width), F32),
            pltpu.VMEM((width, width), F32),
            pltpu.VMEM((group, width, width), F32),
            pltpu.VMEM((heads, width, width), F32),
            pltpu.VMEM((steps, uw, group * tok), BF16),
            pltpu.VMEM((steps, planes, uw, CORES * rows), BF16),
            pltpu.VMEM((steps, planes, CORES, uw, rows), BF16),
            pltpu.VMEM((steps, uw, CORES * rows), F32),
            dma((planes,)),
            dma((chips, planes)),
            dma((chips, planes)),
            dma((chips, planes)),
            dma((chips, planes)),
            dma((heads,)),
            dma((heads,)),
            dma,
            dma,
            dma((2,)),
            dma,
            dma((group,)),
            dma((heads,)),
            dma((steps, group)),
            dma((steps, group)),
            dma((steps, planes, CORES)),
            dma((steps, planes, CORES)),
        ],
        compiler_params=pltpu.CompilerParams(
            collective_id=0, has_side_effects=True, vmem_limit_bytes=56 * 1024 * 1024
        ),
    )(query_rows, key_rows, value_rows, beta.T, norm_gain.reshape(1, -1), out_cotangent)
    return pl.pallas_call(
        hand_over,
        out_shape=(
            jax.ShapeDtypeStruct(attended.shape, BF16),
            jax.ShapeDtypeStruct(weight_grad.shape, F32),
        ),
        in_specs=[vmem] * 2,
        out_specs=(vmem, vmem),
    )(attended, weight_grad)


def solution(mesh):
    spec = P("ctx", "head")
    return jax.shard_map(
        functools.partial(on_device, mesh.shape["ctx"], mesh.shape["head"]),
        mesh=mesh,
        in_specs=(spec, spec, spec, spec, P(), spec),
        out_specs=(spec, spec),
        check_vma=False,
    )
```
